256 devices in a mesh: seq: 4 (over x), head: 64 (over z, y, core).
Axes of the slice: x: 4, y: 4, z: 8, core: 2. Of those that a mesh axis runs over, the one named last changes fastest.
Arguments:
- queries: bfloat16 [2048, 40960], P(('seq', 'head'))
- keys: bfloat16 [2048, 40960], P(('seq', 'head'))
- values: bfloat16 [2048, 40960], P(('seq', 'head')), may hold values from -6 to 6
- block_mask: int32 [64, 16, 9], P('head'), may hold values 0 or 1
- prompt_lengths: int32 [4], replicated, may hold values from 1 to 1024, 2048 in all
Outputs:
- attended: bfloat16 [2048, 40960], P(('seq', 'head'))
The draws below stay inside these ranges and needn't reach their ends.
Inputs may be any that keep to these rules, and one draw needn't show every extreme that they name: `prompt_lengths`: the lengths sum to 2048; the longest prompt has exactly 1024 tokens.
All inputs are finite; a program needn't handle non-finite values. No bound on the sum of `block_mask` on one device may be relied on, other than what follows from the above.
Results may differ from the reference program's by a relative error of at most 0.009.
Values may be sent and summed in bfloat16 or wider, within the bound.
No kernel may reach another device: no remote copies, remote signals or barrier semaphores. Data moves between devices by JAX's collectives and lax.ppermute only.
A program may use at most 64 MiB of HBM per device.

```python
import math
import jax
import jax.numpy as jnp
import numpy as np
from jax import lax

HEAD_DIM = 128
HEADS_DEV = 5
BLOCK = 128
PROMPTS = 4
REACH = 4
SPAN = 9
HEADS = 320
COLS = 40960
TOKENS = 2048
NB = 16
GROUPS = 64


def draw_keys(key, part):
    key = jax.random.fold_in(key, 1)
    base = jnp.clip(jax.random.normal(key, (TOKENS, COLS), jnp.float32), -5.5, 5.5)
    return base.astype(jnp.bfloat16)


def draw_queries(key, part):
    key = jax.random.fold_in(key, 2)
    base = jnp.clip(jax.random.normal(key, (TOKENS, COLS), jnp.float32), -5.5, 5.5)
    return base.astype(jnp.bfloat16)


def place_ends(values, own_key, smallest, largest):
    dims = values.shape
    spot = [jax.random.randint(jax.random.fold_in(own_key, axis), (), 0, dims[axis]) for axis in range(len(dims))]
    values = values.at[tuple(spot)].set(smallest)
    longest = dims.index(max(dims))
    spot[longest] = (spot[longest] + 1) % dims[longest]
    return values.at[tuple(spot)].set(largest)


def steps_of(rng, dims, cuts, smallest, top_value):
    def one(axis_at, blocks):
        heights = jax.random.uniform(jax.random.fold_in(jax.random.fold_in(rng, 6), axis_at), (blocks,), jnp.float32, smallest / len(cuts), top_value / len(cuts))
        return jnp.repeat(jnp.exp(heights), dims[axis_at] // blocks).reshape((-1,) + (1,) * (len(dims) - axis_at - 1))

    gain = one(*cuts[0])
    for cut in cuts[1:]:
        gain = gain * one(*cut)
    return gain


def split_up(amount, total, most, skew):
    loads = [(1 << 20) // math.isqrt(rank ** skew) + 1 for rank in range(2, amount + 1)]
    surplus, holding = total - most - (amount - 1), [1] * (amount - 1)
    while surplus > 0:
        free = [i for i in range(amount - 1) if holding[i] < most]
        pool, budget = sum([loads[i] for i in free]), surplus
        for i in free:
            more = min(most - holding[i], max(1, budget * loads[i] // pool), surplus)
            holding[i] = holding[i] + more
            surplus = surplus - more
    return np.array([most] + holding)


def ragged_sizes(own_key, number_of, total, limit, skew):
    if number_of == 2:
        one = jax.random.randint(own_key, (), max(1, total - limit), min(limit, total - 1) + 1)
        return jnp.stack([one, total - one])
    sizes = jnp.asarray(split_up(number_of, total, limit, skew), jnp.int32)
    couples = (number_of - 1) // 2
    source_of, taker = sizes[1:1 + 2 * couples:2], sizes[2:2 + 2 * couples:2]
    room = jnp.minimum(source_of - 1, limit - taker)
    passed = jax.random.randint(jax.random.fold_in(own_key, 1), (couples,), 0, 1 << 20) % (room + 1)
    sizes = sizes.at[1:1 + 2 * couples:2].set(source_of - passed).at[2:2 + 2 * couples:2].set(taker + passed)
    return sizes[jax.random.permutation(jax.random.fold_in(own_key, 2), number_of)]


def gaussian(key, extent, deviation, limit, split=(), kind=jnp.bfloat16):
    values = jax.random.normal(key, extent, jnp.float32) * deviation
    if len(split) > 0:
        values = steps_of(key, extent, split, -0.22, 0.18) * values
    return jnp.clip(values, min=-limit, max=limit).astype(kind)


def setup_inputs(seed: int = 0) -> dict:
    key_of = jax.random.split(jax.random.key(seed), 6)
    queries = draw_queries(jax.random.fold_in(key_of[5], 71), 0)
    keys = draw_keys(jax.random.fold_in(key_of[5], 71), 0)
    values = gaussian(key_of[2], (TOKENS, COLS), 1.0, 6.0, ((0, 256),))
    block_mask = place_ends((jax.random.randint(key_of[3], (GROUPS, NB, SPAN), 0, 3) < 1).astype(jnp.int32), jax.random.fold_in(key_of[3], 1), 0, 1)
    prompt_lengths = ragged_sizes(key_of[4], PROMPTS, TOKENS, TOKENS // 2, 2).astype(jnp.int32)
    return {"queries": queries, "keys": keys, "values": values, "block_mask": block_mask, "prompt_lengths": prompt_lengths}


neg_big = -1.0e30


def segment_of(positions, ends):
    return jnp.sum((positions[:, None] >= ends[None, :]).astype(jnp.int32), axis=1)


def reference(queries, keys, values, block_mask, prompt_lengths):
    ends = jnp.cumsum(prompt_lengths)[:-1]
    scale = 1.0 / (HEAD_DIM ** 0.5)
    pad = REACH * BLOCK
    window = SPAN * BLOCK
    offsets = jnp.arange(window, dtype=jnp.int32) // BLOCK

    def head_fn(head):
        start = (head * HEAD_DIM).astype(jnp.int32)
        q_head = lax.dynamic_slice_in_dim(queries, start, HEAD_DIM, 1)
        k_head = jnp.pad(lax.dynamic_slice_in_dim(keys, start, HEAD_DIM, 1), ((pad, pad), (0, 0)))
        v_head = jnp.pad(lax.dynamic_slice_in_dim(values, start, HEAD_DIM, 1), ((pad, pad), (0, 0)))
        mask_group = block_mask[head // HEADS_DEV]

        def block_fn(block):
            row_start = (block * BLOCK).astype(jnp.int32)
            q_rows = lax.dynamic_slice_in_dim(q_head, row_start, BLOCK, 0)
            k_rows = lax.dynamic_slice_in_dim(k_head, row_start, window, 0)
            v_rows = lax.dynamic_slice_in_dim(v_head, row_start, window, 0)
            q_pos = row_start + jnp.arange(BLOCK, dtype=jnp.int32)
            k_pos = row_start - pad + jnp.arange(window, dtype=jnp.int32)
            valid = (k_pos >= 0) & (k_pos < TOKENS)
            q_seg = segment_of(q_pos, ends)
            k_seg = segment_of(k_pos, ends)
            block_ok = (mask_group[block][offsets] == 1) | (offsets == REACH)
            allowed = (q_seg[:, None] == k_seg[None, :]) & (block_ok & valid)[None, :]
            scores = jnp.dot(q_rows, k_rows.T, preferred_element_type=jnp.float32) * scale
            scores = jnp.where(allowed, scores, neg_big)
            rowmax = jnp.max(scores, axis=1)
            weights = jnp.where(allowed, jnp.exp(scores - rowmax[:, None]), 0.0)
            total = jnp.sum(weights, axis=1)
            mixed = jnp.dot(weights.astype(jnp.bfloat16), v_rows, preferred_element_type=jnp.float32)
            return (mixed / total[:, None]).astype(jnp.bfloat16)

        blocks = lax.map(block_fn, jnp.arange(NB, dtype=jnp.int32))
        return blocks.reshape(TOKENS, HEAD_DIM)

    heads = lax.map(head_fn, jnp.arange(HEADS, dtype=jnp.int32))
    return jnp.transpose(heads, (1, 0, 2)).reshape(TOKENS, COLS)
```

```python
import functools

import jax
import jax.numpy as jnp
from jax import lax
from jax.experimental import pallas as pl
from jax.experimental.pallas import tpu as pltpu
from jax.sharding import PartitionSpec as P

HEAD_DIM = 128
BLOCK = 128
neg_big = -1e30


def segment_of(positions, ends):
    seg = jnp.zeros_like(positions)
    for end in ends:
        seg = seg + (positions >= end).astype(jnp.int32)
    return seg


def attend_kernel(reach, tokens_all, lengths, first_ref, mask_ref, q_ref, kv_ref, left_ref, right_ref, out_ref):
    rows, cols = q_ref.shape
    heads = cols // HEAD_DIM
    blocks = rows // BLOCK
    span = 2 * reach + 1
    scale = 1.0 / HEAD_DIM**0.5
    first = first_ref[0]
    ends = []
    total = lengths[0]
    for i in range(1, lengths.shape[0]):
        ends.append(total)
        total = total + lengths[i]
    for b in range(blocks):
        q_pos = first + b * BLOCK + lax.broadcasted_iota(jnp.int32, (BLOCK, 1), 0)
        q_seg = segment_of(q_pos, ends)
        q_block = first // BLOCK + b
        bias = []
        for r in range(span):
            k_pos = first + (b + r - reach) * BLOCK + lax.broadcasted_iota(jnp.int32, (1, BLOCK), 1)
            k_seg = segment_of(k_pos, ends)
            k_block = q_block + r - reach
            ok = (k_block >= 0) & (k_block < tokens_all // BLOCK)
            if r != reach:
                ok = ok & (mask_ref[0, q_block, r] == 1)
            k_seg = jnp.where(ok, k_seg, -1)
            bias.append(jnp.where(q_seg == k_seg, 0.0, neg_big))
        bias = jnp.concatenate(bias, axis=1)
        here = slice(b * BLOCK, (b + 1) * BLOCK)
        parts = ((left_ref, slice(b * BLOCK, rows)), (kv_ref, slice(0, rows)), (right_ref, slice(0, (b + 1) * BLOCK)))
        for h in range(heads):
            k_cols = slice(h * HEAD_DIM, (h + 1) * HEAD_DIM)
            v_cols = slice(cols + h * HEAD_DIM, cols + (h + 1) * HEAD_DIM)
            q = q_ref[here, k_cols]
            scores = jnp.concatenate(
                [
                    lax.dot_general(
                        q, ref[part, k_cols], (((1,), (1,)), ((), ())), preferred_element_type=jnp.float32
                    )
                    for ref, part in parts
                ],
                axis=1,
            )
            scores = scores * scale + bias
            row_max = jnp.max(scores, axis=1, keepdims=True)
            weights = jnp.exp(scores - row_max)
            sums = jnp.sum(weights, axis=1, keepdims=True)
            weights = weights.astype(jnp.bfloat16)
            mixed = jnp.zeros((BLOCK, HEAD_DIM), jnp.float32)
            at = 0
            for ref, part in parts:
                width = part.stop - part.start
                mixed = mixed + jnp.dot(
                    weights[:, at : at + width], ref[part, v_cols], preferred_element_type=jnp.float32
                )
                at += width
            out_ref[here, k_cols] = (mixed / sums).astype(jnp.bfloat16)


def attend(prompt_lengths, first, block_mask, q, kv, left, right):
    reach = (block_mask.shape[2] - 1) // 2
    tokens_all = block_mask.shape[1] * BLOCK
    smem = pl.BlockSpec(memory_space=pltpu.SMEM)
    vmem = pl.BlockSpec(memory_space=pltpu.VMEM)
    return pl.pallas_call(
        functools.partial(attend_kernel, reach, tokens_all),
        out_shape=jax.ShapeDtypeStruct(q.shape, q.dtype),
        in_specs=[smem, smem, smem, vmem, vmem, vmem, vmem],
        out_specs=vmem,
        compiler_params=pltpu.CompilerParams(vmem_limit_bytes=40 * 1024 * 1024),
        cost_estimate=pl.CostEstimate(flops=1500000000, bytes_accessed=6000000, transcendentals=3000000),
    )(prompt_lengths, first, block_mask, q, kv, left, right)


def body(queries, keys, values, block_mask, prompt_lengths):
    groups = lax.axis_size("head")
    tokens, cols = queries.shape
    width = cols // groups
    both = jnp.concatenate(
        [keys.reshape(tokens, groups, width), values.reshape(tokens, groups, width)], axis=2
    ).reshape(tokens, 2 * cols)
    kv = lax.all_to_all(both, "head", split_axis=1, concat_axis=0, tiled=True)
    count = lax.axis_size("seq")
    left = lax.ppermute(kv, "seq", [(i, (i + 1) % count) for i in range(count)])
    right = lax.ppermute(kv, "seq", [((i + 1) % count, i) for i in range(count)])
    q = lax.all_to_all(queries, "head", split_axis=1, concat_axis=0, tiled=True)
    first = (lax.axis_index("seq") * q.shape[0]).astype(jnp.int32).reshape(1)
    mixed = attend(prompt_lengths, first, block_mask, q, kv, left, right)
    return lax.all_to_all(mixed, "head", split_axis=0, concat_axis=1, tiled=True)


def solution(mesh):
    placed = (
        P(("seq", "head"), None),
        P(("seq", "head"), None),
        P(("seq", "head"), None),
        P("head", None, None),
        P(),
    )
    return jax.shard_map(
        body, mesh=mesh, in_specs=placed, out_specs=P(("seq", "head"), None), check_vma=False
    )
```

```python
import functools

import jax
import jax.numpy as jnp
from jax import lax
from jax.experimental import pallas as pl
from jax.experimental.pallas import tpu as pltpu
from jax.sharding import PartitionSpec as P

HEAD_DIM = 128
BLOCK = 128
LOG2_E = 1.4426950408889634
neg_big = -1e30


def segment_of(positions, ends):
    seg = jnp.zeros_like(positions)
    for end in ends:
        seg = seg + (positions >= end).astype(jnp.int32)
    return seg


def mask_kernel(reach, tokens_all, lengths, first_ref, mask_ref, bias_ref):
    rows = bias_ref.shape[0]
    first = first_ref[0]
    ends = []
    total = lengths[0]
    for i in range(1, lengths.shape[0]):
        ends.append(total)
        total = total + lengths[i]
    for b in range(rows // BLOCK):
        q_pos = first + b * BLOCK + lax.broadcasted_iota(jnp.int32, (BLOCK, 1), 0)
        q_seg = segment_of(q_pos, ends)
        q_block = first // BLOCK + b
        for r in range(2 * reach + 1):
            k_pos = first + (b + r - reach) * BLOCK + lax.broadcasted_iota(jnp.int32, (1, BLOCK), 1)
            k_seg = segment_of(k_pos, ends)
            k_block = q_block + r - reach
            ok = (k_block >= 0) & (k_block < tokens_all // BLOCK)
            if r != reach:
                ok = ok & (mask_ref[0, q_block, r] == 1)
            k_seg = jnp.where(ok, k_seg, -1)
            bias_ref[b * BLOCK : (b + 1) * BLOCK, r * BLOCK : (r + 1) * BLOCK] = jnp.where(
                q_seg == k_seg, 0.0, neg_big
            )


def attend_kernel(bias_ref, q_ref, kv_ref, left_ref, right_ref, out_ref):
    rows, cols = q_ref.shape
    factor = LOG2_E / HEAD_DIM**0.5
    items = [(b, h) for b in range(rows // BLOCK) for h in range(cols // HEAD_DIM)]

    def here(b):
        return slice(b * BLOCK, (b + 1) * BLOCK)

    def parts(b):
        return (
            (left_ref, slice(b * BLOCK, rows)),
            (kv_ref, slice(0, rows)),
            (right_ref, slice(0, (b + 1) * BLOCK)),
        )

    def score(b, h):
        at = slice(h * HEAD_DIM, (h + 1) * HEAD_DIM)
        q = q_ref[here(b), at]
        products = [
            lax.dot_general(q, ref[part, at], (((1,), (1,)), ((), ())), preferred_element_type=jnp.float32)
            for ref, part in parts(b)
        ]
        return jnp.concatenate(products, axis=1) + bias_ref[here(b), :]

    def weigh(scores):
        row_max = jnp.max(scores, axis=1, keepdims=True)
        weights = jnp.exp2((scores - row_max) * factor)
        return weights.astype(jnp.bfloat16), jnp.sum(weights, axis=1, keepdims=True)

    def mix(b, h, weights, sums):
        at = slice(cols + h * HEAD_DIM, cols + (h + 1) * HEAD_DIM)
        mixed = jnp.zeros((BLOCK, HEAD_DIM), jnp.float32)
        seen = 0
        for ref, part in parts(b):
            width = part.stop - part.start
            mixed = mixed + jnp.dot(
                weights[:, seen : seen + width], ref[part, at], preferred_element_type=jnp.float32
            )
            seen += width
        out_ref[here(b), h * HEAD_DIM : (h + 1) * HEAD_DIM] = (mixed / sums).astype(jnp.bfloat16)

    scored = {0: score(*items[0])}
    weighed = {}
    for i in range(len(items) + 1):
        if i + 1 < len(items):
            scored[i + 1] = score(*items[i + 1])
        if i < len(items):
            weighed[i] = weigh(scored.pop(i))
        if i > 0:
            mix(*items[i - 1], *weighed.pop(i - 1))


smem = pl.BlockSpec(memory_space=pltpu.SMEM)
vmem = pl.BlockSpec(memory_space=pltpu.VMEM)


def mask_bias(prompt_lengths, first, block_mask, rows):
    span = block_mask.shape[2]
    return pl.pallas_call(
        functools.partial(mask_kernel, (span - 1) // 2, block_mask.shape[1] * BLOCK),
        out_shape=jax.ShapeDtypeStruct((rows, span * BLOCK), jnp.float32),
        in_specs=[smem, smem, smem],
        out_specs=vmem,
        compiler_params=pltpu.CompilerParams(vmem_limit_bytes=12 * 1024 * 1024),
        cost_estimate=pl.CostEstimate(flops=3000000, bytes_accessed=2400000, transcendentals=0),
    )(prompt_lengths, first, block_mask)


def attend(bias, q, kv, left, right):
    return pl.pallas_call(
        attend_kernel,
        out_shape=jax.ShapeDtypeStruct(q.shape, q.dtype),
        in_specs=[vmem] * 5,
        out_specs=vmem,
        compiler_params=pltpu.CompilerParams(vmem_limit_bytes=12 * 1024 * 1024),
        cost_estimate=pl.CostEstimate(flops=1500000000, bytes_accessed=6000000, transcendentals=3000000),
    )(bias, q, kv, left, right)


def body(queries, keys, values, block_mask, prompt_lengths):
    groups = lax.axis_size("head")
    tokens, cols = queries.shape
    width = cols // groups
    both = jnp.concatenate(
        [keys.reshape(tokens, groups, width), values.reshape(tokens, groups, width)], axis=2
    ).reshape(tokens, 2 * cols)
    kv = lax.all_to_all(both, "head", split_axis=1, concat_axis=0, tiled=True)
    count = lax.axis_size("seq")
    left = lax.ppermute(kv, "seq", [(i, (i + 1) % count) for i in range(count)])
    right = lax.ppermute(kv, "seq", [((i + 1) % count, i) for i in range(count)])
    q = lax.all_to_all(queries, "head", split_axis=1, concat_axis=0, tiled=True)
    first = (lax.axis_index("seq") * q.shape[0]).astype(jnp.int32).reshape(1)
    bias = mask_bias(prompt_lengths, first, block_mask, q.shape[0])
    mixed = attend(bias, q, kv, left, right)
    return lax.all_to_all(mixed, "head", split_axis=0, concat_axis=1, tiled=True)


def solution(mesh):
    placed = (
        P(("seq", "head"), None),
        P(("seq", "head"), None),
        P(("seq", "head"), None),
        P("head", None, None),
        P(),
    )
    return jax.shard_map(
        body, mesh=mesh, in_specs=placed, out_specs=P(("seq", "head"), None), check_vma=False
    )
```

```python
import functools

import jax
import jax.numpy as jnp
from jax import lax
from jax.experimental import pallas as pl
from jax.experimental.pallas import tpu as pltpu
from jax.sharding import PartitionSpec as P

HEAD_DIM = 128
BLOCK = 128
LOG2_E = 1.4426950408889634
neg_big = -1e30

smem = pl.BlockSpec(memory_space=pltpu.SMEM)
vmem = pl.BlockSpec(memory_space=pltpu.VMEM)


def segment_of(positions, ends):
    seg = jnp.zeros_like(positions)
    for end in ends:
        seg = seg + (positions >= end).astype(jnp.int32)
    return seg


def window_segments(reach, blocks_all, lengths, mask_ref, block):
    ends = []
    total = lengths[0]
    for i in range(1, lengths.shape[0]):
        ends.append(total)
        total = total + lengths[i]
    rows = segment_of(block * BLOCK + lax.broadcasted_iota(jnp.int32, (BLOCK, 1), 0), ends)
    keys = []
    for r in range(2 * reach + 1):
        other = block + r - reach
        ok = (other >= 0) & (other < blocks_all)
        if r != reach:
            ok = ok & (mask_ref[r, 0, block] == 1)
        pos = other * BLOCK + lax.broadcasted_iota(jnp.int32, (1, BLOCK), 1)
        keys.append(jnp.where(ok, segment_of(pos, ends), -1))
    return rows.astype(jnp.float32), jnp.concatenate(keys, axis=1).astype(jnp.float32)


def bias_of(rows, keys):
    return jnp.where(rows == keys, 0.0, neg_big)


def pipelined(items, score, weigh, mix):
    scored = {0: score(*items[0])}
    weighed = {}
    for i in range(len(items) + 1):
        if i + 1 < len(items):
            scored[i + 1] = score(*items[i + 1])
        if i < len(items):
            weighed[i] = weigh(*items[i], scored.pop(i))
        if i > 0:
            mix(*items[i - 1], *weighed.pop(i - 1))


def product(q, k):
    return lax.dot_general(q, k, (((1,), (1,)), ((), ())), preferred_element_type=jnp.float32)


def bias_kernel(reach, blocks_all, lengths, mask_ref, bias_ref):
    blocks = bias_ref.shape[0] // BLOCK
    first = lax.axis_index("seq") * blocks
    for b in range(blocks):
        bias_ref[b * BLOCK : (b + 1) * BLOCK, :] = bias_of(
            *window_segments(reach, blocks_all, lengths, mask_ref, first + b)
        )


def attend_kernel(bias_ref, q_ref, kv_ref, left_ref, right_ref, out_ref):
    rows, cols = q_ref.shape
    blocks = rows // BLOCK
    factor = LOG2_E / HEAD_DIM**0.5

    def here(b):
        return slice(b * BLOCK, (b + 1) * BLOCK)

    def parts(b):
        return (
            (left_ref, slice(b * BLOCK, rows)),
            (kv_ref, slice(0, rows)),
            (right_ref, slice(0, (b + 1) * BLOCK)),
        )

    def score(b, h):
        at = slice(h * HEAD_DIM, (h + 1) * HEAD_DIM)
        q = q_ref[here(b), at]
        return jnp.concatenate([product(q, ref[part, at]) for ref, part in parts(b)], axis=1) + bias_ref[here(b), :]

    def weigh(b, h, scores):
        row_max = jnp.max(scores, axis=1, keepdims=True)
        weights = jnp.exp2((scores - row_max) * factor)
        return weights.astype(jnp.bfloat16), jnp.sum(weights, axis=1, keepdims=True)

    def mix(b, h, weights, sums):
        at = slice(cols + h * HEAD_DIM, cols + (h + 1) * HEAD_DIM)
        mixed = jnp.zeros((BLOCK, HEAD_DIM), jnp.float32)
        seen = 0
        for ref, part in parts(b):
            width = part.stop - part.start
            mixed = mixed + jnp.dot(
                weights[:, seen : seen + width], ref[part, at], preferred_element_type=jnp.float32
            )
            seen += width
        out_ref[here(b), h * HEAD_DIM : (h + 1) * HEAD_DIM] = (mixed / sums).astype(jnp.bfloat16)

    pipelined([(b, h) for b in range(blocks) for h in range(cols // HEAD_DIM)], score, weigh, mix)


def mask_bias(prompt_lengths, block_mask, rows):
    _, blocks_all, span = block_mask.shape
    return pl.pallas_call(
        functools.partial(bias_kernel, (span - 1) // 2, blocks_all),
        out_shape=jax.ShapeDtypeStruct((rows, span * BLOCK), jnp.float32),
        in_specs=[smem, smem],
        out_specs=vmem,
        compiler_params=pltpu.CompilerParams(vmem_limit_bytes=4 * 1024 * 1024),
        cost_estimate=pl.CostEstimate(flops=3000000, bytes_accessed=2400000, transcendentals=0),
    )(prompt_lengths, block_mask.transpose(2, 0, 1))


def attend(bias, q, kv, left, right):
    return pl.pallas_call(
        attend_kernel,
        out_shape=jax.ShapeDtypeStruct(q.shape, q.dtype),
        in_specs=[vmem] * 5,
        out_specs=vmem,
        compiler_params=pltpu.CompilerParams(vmem_limit_bytes=12 * 1024 * 1024),
        cost_estimate=pl.CostEstimate(flops=1500000000, bytes_accessed=6000000, transcendentals=3000000),
    )(bias, q, kv, left, right)


def body(queries, keys, values, block_mask, prompt_lengths):
    groups = lax.axis_size("head")
    count = lax.axis_size("seq")
    tokens, cols = queries.shape
    width = cols // groups
    both = jnp.concatenate(
        [keys.reshape(tokens, groups, width), values.reshape(tokens, groups, width)], axis=2
    ).reshape(tokens, 2 * cols)
    kv = lax.all_to_all(both, "head", split_axis=1, concat_axis=0, tiled=True)
    left = lax.ppermute(kv, "seq", [(i, (i + 1) % count) for i in range(count)])
    right = lax.ppermute(kv, "seq", [((i + 1) % count, i) for i in range(count)])
    q = lax.all_to_all(queries, "head", split_axis=1, concat_axis=0, tiled=True)
    prompt_lengths, q = lax.optimization_barrier((prompt_lengths, q))
    bias = mask_bias(prompt_lengths, block_mask, q.shape[0])
    mixed = attend(bias, q, kv, left, right)
    return lax.all_to_all(mixed, "head", split_axis=0, concat_axis=1, tiled=True)


def solution(mesh):
    placed = (
        P(("seq", "head"), None),
        P(("seq", "head"), None),
        P(("seq", "head"), None),
        P("head", None, None),
        P(),
    )
    return jax.shard_map(
        body, mesh=mesh, in_specs=placed, out_specs=P(("seq", "head"), None), check_vma=False
    )
```

```python
import functools

import jax
import jax.numpy as jnp
from jax import lax
from jax.experimental import pallas as pl
from jax.experimental.pallas import tpu as pltpu
from jax.sharding import PartitionSpec as P

HEAD_DIM = 128
BLOCK = 128
LOG2_E = 1.4426950408889634
neg_big = -1e30

smem = pl.BlockSpec(memory_space=pltpu.SMEM)
vmem = pl.BlockSpec(memory_space=pltpu.VMEM)


def segment_of(positions, ends):
    seg = jnp.zeros_like(positions)
    for end in ends:
        seg = seg + (positions >= end).astype(jnp.int32)
    return seg


def window_segments(reach, blocks_all, lengths, mask_ref, block):
    ends = []
    total = lengths[0]
    for i in range(1, lengths.shape[0]):
        ends.append(total)
        total = total + lengths[i]
    rows = segment_of(block * BLOCK + lax.broadcasted_iota(jnp.int32, (BLOCK, 1), 0), ends)
    keys = []
    for r in range(2 * reach + 1):
        other = block + r - reach
        ok = (other >= 0) & (other < blocks_all)
        if r != reach:
            ok = ok & (mask_ref[r, 0, block] == 1)
        pos = other * BLOCK + lax.broadcasted_iota(jnp.int32, (1, BLOCK), 1)
        keys.append(jnp.where(ok, segment_of(pos, ends), -1))
    return rows.astype(jnp.float32), jnp.concatenate(keys, axis=1).astype(jnp.float32)


def bias_of(rows, keys):
    return jnp.where(rows == keys, 0.0, neg_big)


def pipelined(items, score, weigh, mix):
    scored = {0: score(*items[0])}
    weighed = {}
    for i in range(len(items) + 1):
        if i + 1 < len(items):
            scored[i + 1] = score(*items[i + 1])
        if i < len(items):
            weighed[i] = weigh(*items[i], scored.pop(i))
        if i > 0:
            mix(*items[i - 1], *weighed.pop(i - 1))


def product(q, k):
    return lax.dot_general(q, k, (((1,), (1,)), ((), ())), preferred_element_type=jnp.float32)


def own_kernel(
    reach, blocks_all, lengths, mask_ref, q_ref, kv_ref, bias_ref, max_ref, sum_ref, mixed_ref
):
    rows, cols = q_ref.shape
    blocks = rows // BLOCK
    factor = LOG2_E / HEAD_DIM**0.5
    first = lax.axis_index("seq") * blocks
    biases = []
    for b in range(blocks):
        bias = bias_of(*window_segments(reach, blocks_all, lengths, mask_ref, first + b))
        start = (reach - b) * BLOCK
        biases.append(bias[:, start : start + rows])
        bias_ref[b * BLOCK : (b + 1) * BLOCK, :] = jnp.concatenate([bias[:, :start], bias[:, start + rows :]], axis=1)

    def here(b):
        return slice(b * BLOCK, (b + 1) * BLOCK)

    def score(b, h):
        at = slice(h * HEAD_DIM, (h + 1) * HEAD_DIM)
        return product(q_ref[here(b), at], kv_ref[:, at]) + biases[b]

    def weigh(b, h, scores):
        at = slice(h * HEAD_DIM, (h + 1) * HEAD_DIM)
        row_max = jnp.max(scores, axis=1, keepdims=True)
        weights = jnp.exp2((scores - row_max) * factor)
        max_ref[here(b), at] = jnp.broadcast_to(row_max, (BLOCK, HEAD_DIM))
        sum_ref[here(b), at] = jnp.broadcast_to(jnp.sum(weights, axis=1, keepdims=True), (BLOCK, HEAD_DIM))
        return (weights.astype(jnp.bfloat16),)

    def mix(b, h, weights):
        at = slice(h * HEAD_DIM, (h + 1) * HEAD_DIM)
        v = kv_ref[:, cols + h * HEAD_DIM : cols + (h + 1) * HEAD_DIM]
        mixed_ref[here(b), at] = jnp.dot(weights, v, preferred_element_type=jnp.float32)

    pipelined([(b, h) for b in range(blocks) for h in range(cols // HEAD_DIM)], score, weigh, mix)


def halo_kernel(bias_ref, max_ref, sum_ref, mixed_ref, q_ref, left_ref, right_ref, out_ref):
    rows, cols = q_ref.shape
    blocks = rows // BLOCK
    factor = LOG2_E / HEAD_DIM**0.5

    def here(b):
        return slice(b * BLOCK, (b + 1) * BLOCK)

    def sides(b):
        return (left_ref, slice(b * BLOCK, rows)), (right_ref, slice(0, (b + 1) * BLOCK))

    def score(b, h):
        at = slice(h * HEAD_DIM, (h + 1) * HEAD_DIM)
        q = q_ref[here(b), at]
        return jnp.concatenate([product(q, ref[part, at]) for ref, part in sides(b)], axis=1) + bias_ref[here(b), :]

    def weigh(b, h, scores):
        at = slice(h * HEAD_DIM, (h + 1) * HEAD_DIM)
        own_max = max_ref[here(b), at]
        row_max = jnp.maximum(own_max, jnp.max(scores, axis=1, keepdims=True))
        share = jnp.exp2((own_max - row_max) * factor)
        copies = scores.shape[1] // HEAD_DIM
        weights = jnp.exp2((scores - jnp.concatenate([row_max] * copies, axis=1)) * factor)
        sums = jnp.sum(weights, axis=1, keepdims=True) + share * sum_ref[here(b), at]
        return weights.astype(jnp.bfloat16), share, sums

    def mix(b, h, weights, share, sums):
        at = slice(h * HEAD_DIM, (h + 1) * HEAD_DIM)
        v_at = slice(cols + h * HEAD_DIM, cols + (h + 1) * HEAD_DIM)
        mixed = mixed_ref[here(b), at] * share
        seen = 0
        for ref, part in sides(b):
            width = part.stop - part.start
            mixed = mixed + jnp.dot(
                weights[:, seen : seen + width], ref[part, v_at], preferred_element_type=jnp.float32
            )
            seen += width
        out_ref[here(b), at] = (mixed / sums).astype(jnp.bfloat16)

    pipelined([(b, h) for b in range(blocks) for h in range(cols // HEAD_DIM)], score, weigh, mix)


def attend_own(prompt_lengths, block_mask, q, kv):
    rows, cols = q.shape
    _, blocks_all, span = block_mask.shape
    part = jax.ShapeDtypeStruct((rows, cols), jnp.float32)
    return pl.pallas_call(
        functools.partial(own_kernel, (span - 1) // 2, blocks_all),
        out_shape=(jax.ShapeDtypeStruct((rows, span * BLOCK - rows), jnp.float32), part, part, part),
        in_specs=[smem, smem, vmem, vmem],
        out_specs=[vmem] * 4,
        compiler_params=pltpu.CompilerParams(vmem_limit_bytes=12 * 1024 * 1024),
        cost_estimate=pl.CostEstimate(flops=1000, bytes_accessed=1000, transcendentals=0),
    )(prompt_lengths, block_mask.transpose(2, 0, 1), q, kv)


def attend_halo(own, q, left, right):
    return pl.pallas_call(
        halo_kernel,
        out_shape=jax.ShapeDtypeStruct(q.shape, q.dtype),
        in_specs=[vmem] * 7,
        out_specs=vmem,
        compiler_params=pltpu.CompilerParams(vmem_limit_bytes=12 * 1024 * 1024),
        cost_estimate=pl.CostEstimate(flops=900000000, bytes_accessed=4000000, transcendentals=1600000),
    )(*own, q, left, right)


def body(queries, keys, values, block_mask, prompt_lengths):
    groups = lax.axis_size("head")
    count = lax.axis_size("seq")
    tokens, cols = queries.shape
    width = cols // groups
    both = jnp.concatenate(
        [keys.reshape(tokens, groups, width), values.reshape(tokens, groups, width)], axis=2
    ).reshape(tokens, 2 * cols)
    kv = lax.all_to_all(both, "head", split_axis=1, concat_axis=0, tiled=True)
    left = lax.ppermute(kv, "seq", [(i, (i + 1) % count) for i in range(count)])
    right = lax.ppermute(kv, "seq", [((i + 1) % count, i) for i in range(count)])
    q = lax.all_to_all(queries, "head", split_axis=1, concat_axis=0, tiled=True)
    prompt_lengths, q = lax.optimization_barrier((prompt_lengths, q))
    own = attend_own(prompt_lengths, block_mask, q, kv)
    mixed = attend_halo(own, q, left, right)
    return lax.all_to_all(mixed, "head", split_axis=0, concat_axis=1, tiled=True)


def solution(mesh):
    placed = (
        P(("seq", "head"), None),
        P(("seq", "head"), None),
        P(("seq", "head"), None),
        P("head", None, None),
        P(),
    )
    return jax.shard_map(
        body, mesh=mesh, in_specs=placed, out_specs=P(("seq", "head"), None), check_vma=False
    )
```

```python
import functools

import jax
import jax.numpy as jnp
from jax import lax
from jax.experimental import pallas as pl
from jax.experimental.pallas import tpu as pltpu
from jax.sharding import PartitionSpec as P

HEAD_DIM = 128
BLOCK = 128
LOG2_E = 1.4426950408889634
neg_big = -1e30

smem = pl.BlockSpec(memory_space=pltpu.SMEM)
vmem = pl.BlockSpec(memory_space=pltpu.VMEM)


def segment_of(positions, ends):
    seg = jnp.zeros_like(positions)
    for end in ends:
        seg = seg + (positions >= end).astype(jnp.int32)
    return seg


def window_segments(reach, blocks_all, lengths, mask_ref, block):
    ends = []
    total = lengths[0]
    for i in range(1, lengths.shape[0]):
        ends.append(total)
        total = total + lengths[i]
    rows = segment_of(block * BLOCK + lax.broadcasted_iota(jnp.int32, (BLOCK, 1), 0), ends)
    keys = []
    for r in range(2 * reach + 1):
        other = block + r - reach
        ok = (other >= 0) & (other < blocks_all)
        if r != reach:
            ok = ok & (mask_ref[r, 0, block] == 1)
        pos = other * BLOCK + lax.broadcasted_iota(jnp.int32, (1, BLOCK), 1)
        keys.append(jnp.where(ok, segment_of(pos, ends), -1))
    return rows.astype(jnp.float32), jnp.concatenate(keys, axis=1).astype(jnp.float32)


def bias_of(rows, keys):
    return jnp.where(rows == keys, 0.0, neg_big)


def pipelined(items, score, weigh, mix):
    scored = {0: score(*items[0]), 1: score(*items[1])}
    weighed = {}
    for i in range(len(items) + 1):
        if i + 2 < len(items):
            scored[i + 2] = score(*items[i + 2])
        if i < len(items):
            weighed[i] = weigh(*items[i], scored.pop(i))
        if i > 0:
            mix(*items[i - 1], *weighed.pop(i - 1))


def product(q, k):
    return lax.dot_general(q, k, (((1,), (1,)), ((), ())), preferred_element_type=jnp.float32)


def own_kernel(
    reach, blocks_all, lengths, mask_ref, q_ref, kv_ref, bias_ref, max_ref, sum_ref, mixed_ref
):
    rows, cols = q_ref.shape
    blocks = rows // BLOCK
    factor = LOG2_E / HEAD_DIM**0.5
    first = lax.axis_index("seq") * blocks
    biases = []
    for b in range(blocks):
        bias = bias_of(*window_segments(reach, blocks_all, lengths, mask_ref, first + b))
        start = (reach - b) * BLOCK
        biases.append(bias[:, start : start + rows])
        bias_ref[b * BLOCK : (b + 1) * BLOCK, :] = jnp.concatenate([bias[:, :start], bias[:, start + rows :]], axis=1)

    def here(b):
        return slice(b * BLOCK, (b + 1) * BLOCK)

    def score(b, h):
        at = slice(h * HEAD_DIM, (h + 1) * HEAD_DIM)
        return product(q_ref[here(b), at], kv_ref[:, at]) + biases[b]

    def weigh(b, h, scores):
        at = slice(h * HEAD_DIM, (h + 1) * HEAD_DIM)
        row_max = jnp.max(scores, axis=1, keepdims=True)
        weights = jnp.exp2((scores - row_max) * factor)
        max_ref[here(b), at] = jnp.broadcast_to(row_max, (BLOCK, HEAD_DIM))
        sum_ref[here(b), at] = jnp.broadcast_to(jnp.sum(weights, axis=1, keepdims=True), (BLOCK, HEAD_DIM))
        return (weights.astype(jnp.bfloat16),)

    def mix(b, h, weights):
        at = slice(h * HEAD_DIM, (h + 1) * HEAD_DIM)
        v = kv_ref[:, cols + h * HEAD_DIM : cols + (h + 1) * HEAD_DIM]
        mixed_ref[here(b), at] = jnp.dot(weights, v, preferred_element_type=jnp.float32)

    pipelined([(b, h) for b in range(blocks) for h in range(cols // HEAD_DIM)], score, weigh, mix)


def halo_kernel(*refs):
    *others, one_ref, two_ref, out_ref = refs
    odd = lax.axis_index("head") % 2

    @pl.when(odd == 0)
    def _():
        add_halo(*others, one_ref, two_ref, out_ref)

    @pl.when(odd == 1)
    def _():
        add_halo(*others, two_ref, one_ref, out_ref)


def add_halo(bias_ref, max_ref, sum_ref, mixed_ref, q_ref, left_ref, right_ref, out_ref):
    rows, cols = q_ref.shape
    blocks = rows // BLOCK
    factor = LOG2_E / HEAD_DIM**0.5

    def here(b):
        return slice(b * BLOCK, (b + 1) * BLOCK)

    def sides(b):
        return (left_ref, slice(b * BLOCK, rows)), (right_ref, slice(0, (b + 1) * BLOCK))

    def score(b, h):
        at = slice(h * HEAD_DIM, (h + 1) * HEAD_DIM)
        q = q_ref[here(b), at]
        return jnp.concatenate([product(q, ref[part, at]) for ref, part in sides(b)], axis=1) + bias_ref[here(b), :]

    def weigh(b, h, scores):
        at = slice(h * HEAD_DIM, (h + 1) * HEAD_DIM)
        own_max = max_ref[here(b), at]
        row_max = jnp.maximum(own_max, jnp.max(scores, axis=1, keepdims=True))
        share = jnp.exp2((own_max - row_max) * factor)
        copies = scores.shape[1] // HEAD_DIM
        weights = jnp.exp2((scores - jnp.concatenate([row_max] * copies, axis=1)) * factor)
        sums = jnp.sum(weights, axis=1, keepdims=True) + share * sum_ref[here(b), at]
        return weights.astype(jnp.bfloat16), share, sums

    def mix(b, h, weights, share, sums):
        at = slice(h * HEAD_DIM, (h + 1) * HEAD_DIM)
        v_at = slice(cols + h * HEAD_DIM, cols + (h + 1) * HEAD_DIM)
        mixed = mixed_ref[here(b), at] * share
        seen = 0
        for ref, part in sides(b):
            width = part.stop - part.start
            mixed = mixed + jnp.dot(
                weights[:, seen : seen + width], ref[part, v_at], preferred_element_type=jnp.float32
            )
            seen += width
        out_ref[here(b), at] = (mixed / sums).astype(jnp.bfloat16)

    pipelined([(b, h) for b in range(blocks) for h in range(cols // HEAD_DIM)], score, weigh, mix)


def attend_own(prompt_lengths, block_mask, q, kv):
    rows, cols = q.shape
    _, blocks_all, span = block_mask.shape
    part = jax.ShapeDtypeStruct((rows, cols), jnp.float32)
    return pl.pallas_call(
        functools.partial(own_kernel, (span - 1) // 2, blocks_all),
        out_shape=(jax.ShapeDtypeStruct((rows, span * BLOCK - rows), jnp.float32), part, part, part),
        in_specs=[smem, smem, vmem, vmem],
        out_specs=[vmem] * 4,
        compiler_params=pltpu.CompilerParams(vmem_limit_bytes=12 * 1024 * 1024),
        cost_estimate=pl.CostEstimate(flops=1000, bytes_accessed=1000, transcendentals=0),
    )(prompt_lengths, block_mask.transpose(2, 0, 1), q, kv)


def attend_halo(own, q, left, right):
    return pl.pallas_call(
        halo_kernel,
        out_shape=jax.ShapeDtypeStruct(q.shape, q.dtype),
        in_specs=[vmem] * 7,
        out_specs=vmem,
        compiler_params=pltpu.CompilerParams(vmem_limit_bytes=12 * 1024 * 1024),
        cost_estimate=pl.CostEstimate(flops=900000000, bytes_accessed=4000000, transcendentals=1600000),
    )(*own, q, left, right)


def body(queries, keys, values, block_mask, prompt_lengths):
    groups = lax.axis_size("head")
    count = lax.axis_size("seq")
    tokens, cols = queries.shape
    width = cols // groups
    both = jnp.concatenate(
        [keys.reshape(tokens, groups, width), values.reshape(tokens, groups, width)], axis=2
    ).reshape(tokens, 2 * cols)
    kv = lax.all_to_all(both, "head", split_axis=1, concat_axis=0, tiled=True)
    one, two = (
        lax.ppermute(
            kv,
            ("seq", "head"),
            [
                (i * groups + g, (i + step * (1 - 2 * (g % 2))) % count * groups + g)
                for i in range(count)
                for g in range(groups)
            ],
        )
        for step in (1, -1)
    )
    q = lax.all_to_all(queries, "head", split_axis=1, concat_axis=0, tiled=True)
    prompt_lengths, q = lax.optimization_barrier((prompt_lengths, q))
    own = attend_own(prompt_lengths, block_mask, q, kv)
    mixed = attend_halo(own, q, one, two)
    return lax.all_to_all(mixed, "head", split_axis=0, concat_axis=1, tiled=True)


def solution(mesh):
    placed = (
        P(("seq", "head"), None),
        P(("seq", "head"), None),
        P(("seq", "head"), None),
        P("head", None, None),
        P(),
    )
    return jax.shard_map(
        body, mesh=mesh, in_specs=placed, out_specs=P(("seq", "head"), None), check_vma=False
    )
```

```python
import functools

import jax
import jax.numpy as jnp
from jax import lax
from jax.experimental import pallas as pl
from jax.experimental.pallas import tpu as pltpu
from jax.sharding import PartitionSpec as P

HEAD_DIM = 128
BLOCK = 128
LOG2_E = 1.4426950408889634
LARGEST = 3.4028234663852886e38

smem = pl.BlockSpec(memory_space=pltpu.SMEM)
vmem = pl.BlockSpec(memory_space=pltpu.VMEM)


def segment_of(positions, ends):
    seg = jnp.zeros_like(positions)
    for end in ends:
        seg = seg + (positions >= end).astype(jnp.int32)
    return seg


def window_segments(reach, blocks_all, lengths, mask_ref, block):
    ends = []
    total = lengths[0]
    for i in range(1, lengths.shape[0]):
        ends.append(total)
        total = total + lengths[i]
    rows = segment_of(block * BLOCK + lax.broadcasted_iota(jnp.int32, (BLOCK, 1), 0), ends)
    keys = []
    for r in range(2 * reach + 1):
        other = block + r - reach
        ok = (other >= 0) & (other < blocks_all)
        if r != reach:
            ok = ok & (mask_ref[r, 0, block] == 1)
        pos = other * BLOCK + lax.broadcasted_iota(jnp.int32, (1, BLOCK), 1)
        keys.append(jnp.where(ok, segment_of(pos, ends), -1))
    return rows.astype(jnp.float32), jnp.concatenate(keys, axis=1).astype(jnp.float32)


def limit_of(rows, keys):
    return jnp.where(rows == keys, LARGEST, -LARGEST)


def pipelined(items, score, weigh, mix):
    scored = {0: score(*items[0]), 1: score(*items[1])}
    weighed = {}
    for i in range(len(items) + 1):
        if i + 2 < len(items):
            scored[i + 2] = score(*items[i + 2])
        if i < len(items):
            weighed[i] = weigh(*items[i], scored.pop(i))
        if i > 0:
            mix(*items[i - 1], *weighed.pop(i - 1))


def product(q, k):
    return lax.dot_general(q, k, (((1,), (1,)), ((), ())), preferred_element_type=jnp.float32)


def own_kernel(
    reach, blocks_all, lengths, mask_ref, q_ref, kv_ref, limit_ref, max_ref, sum_ref, mixed_ref
):
    rows, cols = q_ref.shape
    blocks = rows // BLOCK
    factor = LOG2_E / HEAD_DIM**0.5
    first = lax.axis_index("seq") * blocks
    limits = []
    for b in range(blocks):
        limit = limit_of(*window_segments(reach, blocks_all, lengths, mask_ref, first + b))
        start = (reach - b) * BLOCK
        limits.append(limit[:, start : start + rows])
        limit_ref[b * BLOCK : (b + 1) * BLOCK, :] = jnp.concatenate([limit[:, :start], limit[:, start + rows :]], axis=1)

    limits = jnp.concatenate(limits, axis=0)

    def score(h):
        at = slice(h * HEAD_DIM, (h + 1) * HEAD_DIM)
        return jnp.minimum(product(q_ref[:, at], kv_ref[:, at]), limits)

    def weigh(h, scores):
        at = slice(h * HEAD_DIM, (h + 1) * HEAD_DIM)
        row_max = jnp.max(scores, axis=1, keepdims=True)
        weights = jnp.exp2((scores - row_max) * factor)
        max_ref[:, at] = jnp.broadcast_to(row_max, (rows, HEAD_DIM))
        sum_ref[:, at] = jnp.broadcast_to(jnp.sum(weights, axis=1, keepdims=True), (rows, HEAD_DIM))
        return (weights.astype(jnp.bfloat16),)

    def mix(h, weights):
        v = kv_ref[:, cols + h * HEAD_DIM : cols + (h + 1) * HEAD_DIM]
        mixed_ref[:, h * HEAD_DIM : (h + 1) * HEAD_DIM] = jnp.dot(weights, v, preferred_element_type=jnp.float32)

    pipelined([(h,) for h in range(cols // HEAD_DIM)], score, weigh, mix)


def halo_kernel(*refs):
    *others, one_ref, two_ref, out_ref = refs
    odd = lax.axis_index("head") % 2

    @pl.when(odd == 0)
    def _():
        add_halo(*others, one_ref, two_ref, out_ref)

    @pl.when(odd == 1)
    def _():
        add_halo(*others, two_ref, one_ref, out_ref)


def add_halo(limit_ref, max_ref, sum_ref, mixed_ref, q_ref, left_ref, right_ref, out_ref):
    rows, cols = q_ref.shape
    blocks = rows // BLOCK
    factor = LOG2_E / HEAD_DIM**0.5

    def here(b):
        return slice(b * BLOCK, (b + 1) * BLOCK)

    def sides(b):
        return (left_ref, slice(b * BLOCK, rows)), (right_ref, slice(0, (b + 1) * BLOCK))

    def score(b, h):
        at = slice(h * HEAD_DIM, (h + 1) * HEAD_DIM)
        q = q_ref[here(b), at]
        products = [product(q, ref[part, at]) for ref, part in sides(b)]
        return jnp.minimum(jnp.concatenate(products, axis=1), limit_ref[here(b), :])

    def weigh(b, h, scores):
        at = slice(h * HEAD_DIM, (h + 1) * HEAD_DIM)
        own_max = max_ref[here(b), at]
        row_max = jnp.maximum(own_max, jnp.max(scores, axis=1, keepdims=True))
        share = jnp.exp2((own_max - row_max) * factor)
        copies = scores.shape[1] // HEAD_DIM
        weights = jnp.exp2((scores - jnp.concatenate([row_max] * copies, axis=1)) * factor)
        sums = jnp.sum(weights, axis=1, keepdims=True) + share * sum_ref[here(b), at]
        return weights.astype(jnp.bfloat16), share, sums

    def mix(b, h, weights, share, sums):
        at = slice(h * HEAD_DIM, (h + 1) * HEAD_DIM)
        v_at = slice(cols + h * HEAD_DIM, cols + (h + 1) * HEAD_DIM)
        mixed = mixed_ref[here(b), at] * share
        seen = 0
        for ref, part in sides(b):
            width = part.stop - part.start
            mixed = mixed + jnp.dot(
                weights[:, seen : seen + width], ref[part, v_at], preferred_element_type=jnp.float32
            )
            seen += width
        out_ref[here(b), at] = (mixed / sums).astype(jnp.bfloat16)

    pipelined([(b, h) for b in range(blocks) for h in range(cols // HEAD_DIM)], score, weigh, mix)


def attend_own(prompt_lengths, block_mask, q, kv):
    rows, cols = q.shape
    _, blocks_all, span = block_mask.shape
    part = jax.ShapeDtypeStruct((rows, cols), jnp.float32)
    return pl.pallas_call(
        functools.partial(own_kernel, (span - 1) // 2, blocks_all),
        out_shape=(jax.ShapeDtypeStruct((rows, span * BLOCK - rows), jnp.float32), part, part, part),
        in_specs=[smem, smem, vmem, vmem],
        out_specs=[vmem] * 4,
        compiler_params=pltpu.CompilerParams(vmem_limit_bytes=12 * 1024 * 1024),
        cost_estimate=pl.CostEstimate(flops=1000, bytes_accessed=1000, transcendentals=0),
    )(prompt_lengths, block_mask.transpose(2, 0, 1), q, kv)


def attend_halo(own, q, left, right):
    return pl.pallas_call(
        halo_kernel,
        out_shape=jax.ShapeDtypeStruct(q.shape, q.dtype),
        in_specs=[vmem] * 7,
        out_specs=vmem,
        compiler_params=pltpu.CompilerParams(vmem_limit_bytes=12 * 1024 * 1024),
        cost_estimate=pl.CostEstimate(flops=900000000, bytes_accessed=4000000, transcendentals=1600000),
    )(*own, q, left, right)


def body(queries, keys, values, block_mask, prompt_lengths):
    groups = lax.axis_size("head")
    count = lax.axis_size("seq")
    tokens, cols = queries.shape
    width = cols // groups
    both = jnp.concatenate(
        [keys.reshape(tokens, groups, width), values.reshape(tokens, groups, width)], axis=2
    ).reshape(tokens, 2 * cols)
    kv = lax.all_to_all(both, "head", split_axis=1, concat_axis=0, tiled=True)
    one, two = (
        lax.ppermute(
            kv,
            ("seq", "head"),
            [
                (i * groups + g, (i + step * (1 - 2 * (g % 2))) % count * groups + g)
                for i in range(count)
                for g in range(groups)
            ],
        )
        for step in (1, -1)
    )
    q = lax.all_to_all(queries, "head", split_axis=1, concat_axis=0, tiled=True)
    prompt_lengths, q = lax.optimization_barrier((prompt_lengths, q))
    own = attend_own(prompt_lengths, block_mask, q, kv)
    mixed = attend_halo(own, q, one, two)
    return lax.all_to_all(mixed, "head", split_axis=0, concat_axis=1, tiled=True)


def solution(mesh):
    placed = (
        P(("seq", "head"), None),
        P(("seq", "head"), None),
        P(("seq", "head"), None),
        P("head", None, None),
        P(),
    )
    return jax.shard_map(
        body, mesh=mesh, in_specs=placed, out_specs=P(("seq", "head"), None), check_vma=False
    )
```

```python
import functools

import jax
import jax.numpy as jnp
from jax import lax
from jax.experimental import pallas as pl
from jax.experimental.pallas import tpu as pltpu
from jax.sharding import PartitionSpec as P

HEAD_DIM = 128
BLOCK = 128
LOG2_E = 1.4426950408889634
LARGEST = 3.4028234663852886e38

smem = pl.BlockSpec(memory_space=pltpu.SMEM)
vmem = pl.BlockSpec(memory_space=pltpu.VMEM)


def segment_of(positions, ends):
    seg = jnp.zeros_like(positions)
    for end in ends:
        seg = seg + (positions >= end).astype(jnp.int32)
    return seg


def window_segments(reach, blocks_all, lengths, mask_ref, block):
    ends = []
    total = lengths[0]
    for i in range(1, lengths.shape[0]):
        ends.append(total)
        total = total + lengths[i]
    rows = segment_of(block * BLOCK + lax.broadcasted_iota(jnp.int32, (BLOCK, 1), 0), ends)
    keys = []
    for r in range(2 * reach + 1):
        other = block + r - reach
        ok = (other >= 0) & (other < blocks_all)
        if r != reach:
            ok = ok & (mask_ref[r, 0, block] == 1)
        pos = other * BLOCK + lax.broadcasted_iota(jnp.int32, (1, BLOCK), 1)
        keys.append(jnp.where(ok, segment_of(pos, ends), -1))
    return rows.astype(jnp.float32), jnp.concatenate(keys, axis=1).astype(jnp.float32)


def limit_of(rows, keys):
    return jnp.where(rows == keys, LARGEST, -LARGEST)


def pipelined(items, score, weigh, mix):
    ahead = 3
    scored = {i: score(*items[i]) for i in range(ahead)}
    weighed = {}
    for i in range(len(items) + 1):
        if i + ahead < len(items):
            scored[i + ahead] = score(*items[i + ahead])
        if i < len(items):
            weighed[i] = weigh(*items[i], scored.pop(i))
        if i > 0:
            mix(*items[i - 1], *weighed.pop(i - 1))


def product(q, k):
    return lax.dot_general(q, k, (((1,), (1,)), ((), ())), preferred_element_type=jnp.float32)


def own_kernel(
    reach, blocks_all, lengths, mask_ref, q_ref, kv_ref, limit_ref, max_ref, sum_ref, mixed_ref
):
    rows, cols = q_ref.shape
    blocks = rows // BLOCK
    factor = LOG2_E / HEAD_DIM**0.5
    first = lax.axis_index("seq") * blocks
    limits = []
    for b in range(blocks):
        limit = limit_of(*window_segments(reach, blocks_all, lengths, mask_ref, first + b))
        start = (reach - b) * BLOCK
        limits.append(limit[:, start : start + rows])
        limit_ref[b * BLOCK : (b + 1) * BLOCK, :] = jnp.concatenate([limit[:, :start], limit[:, start + rows :]], axis=1)

    limits = jnp.concatenate(limits, axis=0)

    def score(h):
        at = slice(h * HEAD_DIM, (h + 1) * HEAD_DIM)
        return jnp.minimum(product(q_ref[:, at], kv_ref[:, at]), limits)

    def weigh(h, scores):
        at = slice(h * HEAD_DIM, (h + 1) * HEAD_DIM)
        row_max = jnp.max(scores, axis=1, keepdims=True)
        weights = jnp.exp2((scores - row_max) * factor)
        max_ref[:, at] = jnp.broadcast_to(row_max, (rows, HEAD_DIM))
        sum_ref[:, at] = jnp.broadcast_to(jnp.sum(weights, axis=1, keepdims=True), (rows, HEAD_DIM))
        return (weights.astype(jnp.bfloat16),)

    def mix(h, weights):
        v = kv_ref[:, cols + h * HEAD_DIM : cols + (h + 1) * HEAD_DIM]
        mixed_ref[:, h * HEAD_DIM : (h + 1) * HEAD_DIM] = jnp.dot(weights, v, preferred_element_type=jnp.float32)

    pipelined([(h,) for h in range(cols // HEAD_DIM)], score, weigh, mix)


def halo_kernel(*refs):
    *others, one_ref, two_ref, out_ref = refs
    odd = lax.axis_index("head") % 2

    @pl.when(odd == 0)
    def _():
        add_halo(*others, one_ref, two_ref, out_ref)

    @pl.when(odd == 1)
    def _():
        add_halo(*others, two_ref, one_ref, out_ref)


def add_halo(limit_ref, max_ref, sum_ref, mixed_ref, q_ref, left_ref, right_ref, out_ref):
    rows, cols = q_ref.shape
    blocks = rows // BLOCK
    factor = LOG2_E / HEAD_DIM**0.5

    def here(b):
        return slice(b * BLOCK, (b + 1) * BLOCK)

    def sides(b):
        return (left_ref, slice(b * BLOCK, rows)), (right_ref, slice(0, (b + 1) * BLOCK))

    def score(b, h):
        at = slice(h * HEAD_DIM, (h + 1) * HEAD_DIM)
        q = q_ref[here(b), at]
        products = [product(q, ref[part, at]) for ref, part in sides(b)]
        return jnp.minimum(jnp.concatenate(products, axis=1), limit_ref[here(b), :])

    def weigh(b, h, scores):
        at = slice(h * HEAD_DIM, (h + 1) * HEAD_DIM)
        own_max = max_ref[here(b), at]
        row_max = jnp.maximum(own_max, jnp.max(scores, axis=1, keepdims=True))
        share = jnp.exp2((own_max - row_max) * factor)
        copies = scores.shape[1] // HEAD_DIM
        weights = jnp.exp2((scores - jnp.concatenate([row_max] * copies, axis=1)) * factor)
        sums = jnp.sum(weights, axis=1, keepdims=True) + share * sum_ref[here(b), at]
        return weights.astype(jnp.bfloat16), share, sums

    def mix(b, h, weights, share, sums):
        at = slice(h * HEAD_DIM, (h + 1) * HEAD_DIM)
        v_at = slice(cols + h * HEAD_DIM, cols + (h + 1) * HEAD_DIM)
        mixed = mixed_ref[here(b), at] * share
        seen = 0
        for ref, part in sides(b):
            width = part.stop - part.start
            mixed = mixed + jnp.dot(
                weights[:, seen : seen + width], ref[part, v_at], preferred_element_type=jnp.float32
            )
            seen += width
        out_ref[here(b), at] = (mixed / sums).astype(jnp.bfloat16)

    pipelined([(b, h) for b in range(blocks) for h in range(cols // HEAD_DIM)], score, weigh, mix)


def attend_own(prompt_lengths, block_mask, q, kv):
    rows, cols = q.shape
    _, blocks_all, span = block_mask.shape
    part = jax.ShapeDtypeStruct((rows, cols), jnp.float32)
    return pl.pallas_call(
        functools.partial(own_kernel, (span - 1) // 2, blocks_all),
        out_shape=(jax.ShapeDtypeStruct((rows, span * BLOCK - rows), jnp.float32), part, part, part),
        in_specs=[smem, smem, vmem, vmem],
        out_specs=[vmem] * 4,
        compiler_params=pltpu.CompilerParams(vmem_limit_bytes=12 * 1024 * 1024),
        cost_estimate=pl.CostEstimate(flops=1000, bytes_accessed=1000, transcendentals=0),
    )(prompt_lengths, block_mask.transpose(2, 0, 1), q, kv)


def attend_halo(own, q, left, right):
    return pl.pallas_call(
        halo_kernel,
        out_shape=jax.ShapeDtypeStruct(q.shape, q.dtype),
        in_specs=[vmem] * 7,
        out_specs=vmem,
        compiler_params=pltpu.CompilerParams(vmem_limit_bytes=12 * 1024 * 1024),
        cost_estimate=pl.CostEstimate(flops=900000000, bytes_accessed=4000000, transcendentals=1600000),
    )(*own, q, left, right)


def body(queries, keys, values, block_mask, prompt_lengths):
    groups = lax.axis_size("head")
    count = lax.axis_size("seq")
    tokens, cols = queries.shape
    width = cols // groups
    both = jnp.concatenate(
        [keys.reshape(tokens, groups, width), values.reshape(tokens, groups, width)], axis=2
    ).reshape(tokens, 2 * cols)
    kv = lax.all_to_all(both, "head", split_axis=1, concat_axis=0, tiled=True)
    one, two = (
        lax.ppermute(
            kv,
            ("seq", "head"),
            [
                (i * groups + g, (i + step * (1 - 2 * (g % 2))) % count * groups + g)
                for i in range(count)
                for g in range(groups)
            ],
        )
        for step in (1, -1)
    )
    q = lax.all_to_all(queries, "head", split_axis=1, concat_axis=0, tiled=True)
    prompt_lengths, q = lax.optimization_barrier((prompt_lengths, q))
    own = attend_own(prompt_lengths, block_mask, q, kv)
    mixed = attend_halo(own, q, one, two)
    return lax.all_to_all(mixed, "head", split_axis=0, concat_axis=1, tiled=True)


def solution(mesh):
    placed = (
        P(("seq", "head"), None),
        P(("seq", "head"), None),
        P(("seq", "head"), None),
        P("head", None, None),
        P(),
    )
    return jax.shard_map(
        body, mesh=mesh, in_specs=placed, out_specs=P(("seq", "head"), None), check_vma=False
    )
```
